32 devices in a mesh: replica: 2 (over y), head: 8 (over z, x), batch: 2 (over core).
Axes of the slice: x: 2, y: 2, z: 4, core: 2. Of those that a mesh axis runs over, the one named last changes fastest.
Arguments:
- residual: bfloat16 [2, 16, 8192], P(None, ('replica', 'batch'), 'head'), parts along dimension 1, may hold values from -4.5 to 4.5
- norm_gain: bfloat16 [8192], P('head'), may hold values from 0.099609375 to 1.8984375
- queries: bfloat16 [2, 32, 4, 8, 128], P(None, ('replica', 'batch', 'head')), parts along dimension 1, may hold values from -140 to 140
- cache_keys: bfloat16 [2, 32, 4, 256, 128], P(None, ('replica', 'batch', 'head')), parts along dimension 1, may hold values from -6 to 6
- cache_values: bfloat16 [2, 32, 4, 256, 128], P(None, ('replica', 'batch', 'head')), parts along dimension 1, may hold values from -6 to 6
- new_keys: bfloat16 [2, 32, 4, 128], P(None, ('replica', 'batch', 'head')), parts along dimension 1, may hold values from -6 to 6
- new_values: bfloat16 [2, 32, 4, 128], P(None, ('replica', 'batch', 'head')), parts along dimension 1, may hold values from -6 to 6
- lengths: int32 [2, 16], P(None, 'replica'), parts along dimension 1, may hold values from 64 to 256, as said below
- out_packed: int32 [4096, 8192], P(None, 'head'), may hold values from 0 to 255
- out_scales: bfloat16 [64, 8192], P(None, 'head'), may hold values from 0.0012130737 to 0.004852295
- ffn_packed: int32 [8192, 32768], P('batch', 'head'), may hold values from 0 to 4095
- gate_scales: bfloat16 [64, 32768], P('batch', 'head'), may hold values from 0.0012130737 to 0.004852295
- up_scales: bfloat16 [64, 32768], P('batch', 'head'), may hold values from 0.0012130737 to 0.004852295
- down_scales: bfloat16 [256, 8192], P('head', 'batch'), may hold values from 0.00060653687 to 0.0024261475
Outputs:
- attn_stream: bfloat16 [2, 16, 8192], P(None, ('replica', 'batch'), 'head'), parts along dimension 1
- ffn_out: bfloat16 [2, 16, 8192], P(None, 'replica', ('batch', 'head')), parts along dimension 1
The draws below stay inside these ranges and needn't reach their ends.
There are 2 independent parts, one for each index of `replica`. The reference program is written for one: setup_inputs(seed, part) draws one part's arguments, and reference() takes and returns one part's arrays. A program takes and returns all parts, laid end to end along the dimension named above; an argument that names none is the same for every part. Nothing has to cross between parts.
Inputs may be any that keep to these rules, and one draw needn't show every extreme that they name: `lengths`: the first sequence of each micro-batch holds all 256 positions.
All inputs are finite; a program needn't handle non-finite values.
Results may differ from the reference program's by a relative error of at most 0.0065.
Values may be sent and summed in bfloat16 or wider, within the bound.
A program may use at most 384 MiB of HBM per device.

```python
import math
import jax
import jax.numpy as jnp
from jax import lax

D = 8192
HEADS = 64
KV_HEADS = 8
HD = 128
FF = 32768
GROUP = 128
MB = 2
LEN = 256
SEQ_DEV = 4
QPER = 8
UNITS = 16
ROWS = 8


def key_heads(key):
    return jnp.clip(jax.random.normal(key, (MB, UNITS, SEQ_DEV, HD), jnp.float32), -6.0, 6.0)


def feature_profile(base, ratio):
    position = jnp.arange(D, dtype=jnp.float32) / (D - 1)
    return base * jnp.exp(position * jnp.log(ratio))


def draw_residual(key, part):
    key = jax.random.fold_in(key, 11)
    profile = feature_profile(0.15, 5.0)
    values = jnp.clip(jax.random.normal(key, (MB, ROWS, D), jnp.float32), -6.0, 6.0)
    return (values * profile[None, None, :]).astype(jnp.bfloat16)


def draw_cache_keys(key, part):
    first = key_heads(key)
    key = jax.random.fold_in(key, 3)
    rest = jnp.clip(jax.random.normal(key, (MB, UNITS, SEQ_DEV, LEN, HD), jnp.float32), -6.0, 6.0)
    rest = rest.at[:, :, :, 0, :].set(first)
    return rest.astype(jnp.bfloat16)


def draw_queries(key, part):
    key = jax.random.fold_in(key, 7)
    base = jnp.clip(jax.random.normal(key, (MB, UNITS, SEQ_DEV, QPER, HD), jnp.float32), -6.0, 6.0)
    return base.astype(jnp.bfloat16)


def draw_lengths(key, part):
    key = jax.random.fold_in(key, 5)
    drawn = jax.random.randint(key, (MB, ROWS), LEN // 4, LEN + 1, dtype=jnp.int32)
    return drawn.at[:, 0].set(LEN)


def touch_ends(result, rng, least, largest):
    dims = result.shape
    spot = [jax.random.randint(jax.random.fold_in(rng, axis), (), 0, dims[axis]) for axis in range(len(dims))]
    result = result.at[tuple(spot)].set(least)
    longest = dims.index(max(dims))
    spot[longest] = (spot[longest] + 1) % dims[longest]
    return result.at[tuple(spot)].set(largest)


def block_scale(stream_key, extent, pieces, smallest, top_value):
    loudness, own = 1.0, jax.random.fold_in(stream_key, 6)
    for dim, shards_of in pieces:
        draws = jnp.exp(jax.random.uniform(jax.random.fold_in(own, dim), (shards_of,), jnp.float32, smallest / len(pieces), top_value / len(pieces)))
        loudness = loudness * jnp.repeat(draws, extent[dim] // shards_of).reshape([-1 if axis == dim else 1 for axis in range(len(extent))])
    return loudness


def centred(own_key, shape, width, most, shards=(), held_as=jnp.bfloat16):
    result = width * jax.random.normal(own_key, shape, jnp.float32)
    if shards:
        result = result * block_scale(own_key, shape, shards, -0.22, 0.18)
    return jnp.clip(result, -most, most).astype(held_as)


def setup_inputs(seed: int = 0, part: int = 0) -> dict:
    streams_of = jax.random.split(jax.random.key(seed), 15)
    part_splits = jax.random.split(jax.random.fold_in(streams_of[14], part), 15)
    residual = draw_residual(jax.random.fold_in(jax.random.fold_in(streams_of[14], part), 71), part)
    norm_gain = jnp.clip(1.0 + 0.18 * jax.random.normal(streams_of[1], (D,), jnp.float32), 0.099609375, 1.8984375).astype(jnp.bfloat16)
    queries = draw_queries(jax.random.fold_in(jax.random.fold_in(streams_of[14], part), 71), part)
    cache_keys = draw_cache_keys(jax.random.fold_in(jax.random.fold_in(streams_of[14], part), 71), part)
    cache_values = centred(part_splits[4], (MB, UNITS, SEQ_DEV, LEN, HD), 1.0, 6.0, ((1, 16),))
    new_keys = centred(part_splits[5], (MB, UNITS, SEQ_DEV, HD), 1.0, 6.0, ((1, 16),))
    new_values = centred(part_splits[6], (MB, UNITS, SEQ_DEV, HD), 1.0, 6.0, ((1, 16),))
    lengths = draw_lengths(jax.random.fold_in(jax.random.fold_in(streams_of[14], part), 71), part)
    out_packed = touch_ends(jax.random.randint(streams_of[8], (HEADS * HD // 2, D), 0, 256), jax.random.fold_in(streams_of[8], 1), 0, 255).astype(jnp.int32)
    out_scales = jnp.clip(jnp.exp(math.log(0.004852295) - 1.3862944 * jax.random.uniform(streams_of[9], (HEADS * HD // GROUP, D), jnp.float32) ** block_scale(streams_of[9], (HEADS * HD // GROUP, D), ((1, 8),), -0.2, 0.2)), 0.0012130737, 0.004852295).astype(jnp.bfloat16)
    ffn_packed = touch_ends(jax.random.randint(streams_of[10], (D, FF), 0, 4096), jax.random.fold_in(streams_of[10], 1), 0, 4095).astype(jnp.int32)
    gate_scales = jnp.clip(jnp.exp(math.log(0.004852295) - 1.3862944 * jax.random.uniform(streams_of[11], (D // GROUP, FF), jnp.float32) ** block_scale(streams_of[11], (D // GROUP, FF), ((0, 2), (1, 8)), -0.2, 0.2)), 0.0012130737, 0.004852295).astype(jnp.bfloat16)
    up_scales = jnp.clip(jnp.exp(math.log(0.004852295) - 1.3862944 * jax.random.uniform(streams_of[12], (D // GROUP, FF), jnp.float32) ** block_scale(streams_of[12], (D // GROUP, FF), ((0, 2), (1, 8)), -0.2, 0.2)), 0.0012130737, 0.004852295).astype(jnp.bfloat16)
    down_scales = jnp.clip(jnp.exp(math.log(0.0024261475) - 1.3862944 * jax.random.uniform(streams_of[13], (FF // GROUP, D), jnp.float32) ** block_scale(streams_of[13], (FF // GROUP, D), ((0, 8), (1, 2)), -0.2, 0.2)), 0.00060653687, 0.0024261475).astype(jnp.bfloat16)
    return dict(residual=residual, norm_gain=norm_gain, queries=queries, cache_keys=cache_keys, cache_values=cache_values, new_keys=new_keys, new_values=new_values, lengths=lengths, out_packed=out_packed, out_scales=out_scales, ffn_packed=ffn_packed, gate_scales=gate_scales, up_scales=up_scales, down_scales=down_scales)


epsilon = 1e-05

def unpack_pairs(packed, scales):
    shifts = 4 * jnp.arange(2, dtype=jnp.int32)
    nibbles = jnp.bitwise_and(jnp.right_shift(packed[:, None, :], shifts[None, :, None]), 15)
    nibbles = nibbles.reshape(packed.shape[0] * 2, packed.shape[1]).astype(jnp.float32) - 8.0
    spread = jnp.repeat(scales.astype(jnp.float32), nibbles.shape[0] // scales.shape[0], axis=0)
    return (nibbles * spread).astype(jnp.bfloat16)

def field_codes(words, shift, scales):
    nibbles = jnp.bitwise_and(jnp.right_shift(words, shift), 15).astype(jnp.float32) - 8.0
    spread = jnp.repeat(scales.astype(jnp.float32), words.shape[0] // scales.shape[0], axis=0)
    return (nibbles * spread).astype(jnp.bfloat16)

def attend(query, keys, values, key_new, value_new, seq_lens):
    scale = HD ** (-0.5)
    scores = jnp.einsum('ske,spe->skp', query.astype(jnp.float32), keys.astype(jnp.float32)) * scale
    score_new = jnp.einsum('ske,se->sk', query.astype(jnp.float32), key_new.astype(jnp.float32)) * scale
    position = jnp.arange(keys.shape[1], dtype=jnp.int32)
    live_mask = position[None, None, :] < seq_lens[:, None, None]
    row_max = jnp.maximum(lax.optimization_barrier(jnp.max(jnp.where(live_mask, scores, -jnp.inf), axis=-1)), score_new)
    weights = jnp.where(live_mask, jnp.exp(scores - row_max[..., None]), 0.0)
    weight_new = jnp.exp(score_new - row_max)
    denominator = lax.optimization_barrier(jnp.sum(weights, axis=-1)) + weight_new
    probs = (weights / denominator[..., None]).astype(jnp.bfloat16)
    prob_new = (weight_new / denominator).astype(jnp.bfloat16)
    mixed = jnp.einsum('skp,spe->ske', probs.astype(jnp.float32), values.astype(jnp.float32))
    mixed = mixed + prob_new.astype(jnp.float32)[..., None] * value_new.astype(jnp.float32)[:, None, :]
    return mixed.astype(jnp.bfloat16).reshape(mixed.shape[0], -1)

def feed_forward(normed, ffn_packed, gate_scales, up_scales, down_scales):
    block_width = min(FF, 2048)
    total = jnp.zeros((normed.shape[0], D), jnp.float32)
    for start in range(0, FF, block_width):
        words = ffn_packed[:, start:start + block_width]
        gate_weight = field_codes(words, 0, gate_scales[:, start:start + block_width])
        up_weight = field_codes(words, 4, up_scales[:, start:start + block_width])
        down_weight = field_codes(words.T, 8, down_scales[start // GROUP:(start + block_width) // GROUP, :])
        gate_sum = jnp.dot(normed, gate_weight, preferred_element_type=jnp.float32)
        up_sum = jnp.dot(normed, up_weight, preferred_element_type=jnp.float32)
        hidden = (jax.nn.silu(gate_sum) * up_sum).astype(jnp.bfloat16)
        total = total + jnp.dot(hidden, down_weight, preferred_element_type=jnp.float32)
    return total.astype(jnp.bfloat16)

def reference(residual, norm_gain, queries, cache_keys, cache_values, new_keys, new_values, lengths, out_packed, out_scales, ffn_packed, gate_scales, up_scales, down_scales):
    blocks = ROWS // SEQ_DEV
    seq_lens = jnp.broadcast_to(lengths.reshape(MB, blocks, 1, SEQ_DEV), (MB, blocks, KV_HEADS, SEQ_DEV)).reshape(MB * UNITS, SEQ_DEV)
    flat = (queries.reshape((MB * UNITS,) + queries.shape[2:]), cache_keys.reshape((MB * UNITS,) + cache_keys.shape[2:]), cache_values.reshape((MB * UNITS,) + cache_values.shape[2:]), new_keys.reshape((MB * UNITS,) + new_keys.shape[2:]), new_values.reshape((MB * UNITS,) + new_values.shape[2:]), seq_lens)
    attended = lax.map(lambda item: attend(*item), flat)
    attended = attended.reshape(MB, blocks, KV_HEADS, SEQ_DEV, QPER * HD)
    attended = jnp.transpose(attended, (0, 1, 3, 2, 4)).reshape(MB * ROWS, HEADS * HD)
    out_weight = unpack_pairs(out_packed, out_scales)
    projected = jnp.dot(attended, out_weight, preferred_element_type=jnp.float32)
    stream = (residual.reshape(MB * ROWS, D).astype(jnp.float32) + projected).astype(jnp.bfloat16)
    stream_f = stream.astype(jnp.float32)
    mean_sq = lax.optimization_barrier(jnp.mean(stream_f * stream_f, axis=-1))
    normed = (stream_f * lax.rsqrt(mean_sq + epsilon)[:, None] * norm_gain.astype(jnp.float32)).astype(jnp.bfloat16)
    branch = feed_forward(normed, ffn_packed, gate_scales, up_scales, down_scales)
    return (stream.reshape(MB, ROWS, D), branch.reshape(MB, ROWS, D))
```

```python
import functools

import jax
import jax.numpy as jnp
from jax import lax
from jax.experimental import pallas as pl
from jax.experimental.pallas import tpu as pltpu
from jax.sharding import PartitionSpec as P

KV_HEADS = 8
GROUP = 128
EPSILON = 1e-05
MESH = pl.DeviceIdType.MESH
F32 = jnp.float32
BF16 = jnp.bfloat16
CHUNK = 256
FTILE = 512
NT = (((1,), (1,)), ((), ()))


def kernel(
    heads,
    blocks,
    res_ref,
    gain_ref,
    q_ref,
    ck_ref,
    cv_ref,
    nk_ref,
    nv_ref,
    len_ref,
    op_ref,
    os_ref,
    fp_ref,
    gs_ref,
    us_ref,
    ds_ref,
    stream_ref,
    out_ref,
    oring,
    ocodes,
    osf,
    gsf,
    usf,
    dsf,
    mix,
    att_mine,
    att_all,
    att_lhs,
    x_mine,
    x_all,
    sq_mine,
    sq_all,
    nbd,
    nsum,
    fring,
    dcodes,
    acc,
    part_send,
    part_recv,
    acc_out,
    rs_send,
    rs_recv,
    osem,
    fsem,
    att_ss,
    att_rs,
    x_ss,
    x_rs,
    sq_ss,
    sq_rs,
    pt_ss,
    pt_rs,
    rd_ss,
    rd_rs,
):
    head = lax.axis_index("head")
    batch = lax.axis_index("batch")
    half = heads // 2
    inst = q_ref.shape[0]
    qper = q_ref.shape[1]
    positions = ck_ref.shape[1]
    rows = res_ref.shape[0]
    width = res_ref.shape[1]
    both = 2 * rows
    feat = fp_ref.shape[0]
    hidden_units = fp_ref.shape[1]
    words = op_ref.shape[0]
    out_slots = oring.shape[0]
    ffn_slots = fring.shape[0]
    out_chunks = words // CHUNK
    kchunks = feat // CHUNK
    ftiles = hidden_units // FTILE
    total_chunks = kchunks * ftiles

    def out_copy(c):
        slot = lax.rem(c, out_slots)
        first = pl.multiple_of(c * CHUNK, CHUNK)
        return pltpu.make_async_copy(
            op_ref.at[pl.ds(first, CHUNK), :], oring.at[slot], osem.at[slot]
        )

    def ffn_copy(c):
        slot = lax.rem(c, ffn_slots)
        j = c // kchunks
        k = lax.rem(c, kchunks)
        return pltpu.make_async_copy(
            fp_ref.at[
                pl.ds(pl.multiple_of(k * CHUNK, CHUNK), CHUNK),
                pl.ds(pl.multiple_of(j * FTILE, FTILE), FTILE),
            ],
            fring.at[slot],
            fsem.at[slot],
        )

    def start_out(c, _):
        out_copy(c).start()
        return 0

    def start_ffn(c, _):
        ffn_copy(c).start()
        return 0

    barrier = pltpu.get_barrier_semaphore()

    def greet(i, _):
        other = lax.rem(head + i, heads)
        pl.semaphore_signal(
            barrier, inc=1, device_id={"head": other, "batch": 1 - batch}, device_id_type=MESH
        )

        @pl.when(i > 0)
        def _():
            pl.semaphore_signal(
                barrier, inc=1, device_id={"head": other, "batch": batch}, device_id_type=MESH
            )

        return 0

    lax.fori_loop(0, heads, greet, 0)
    lax.fori_loop(0, out_slots, start_out, 0)
    lax.fori_loop(0, ffn_slots, start_ffn, 0)

    scale = q_ref.shape[2] ** (-0.5)
    new_k = nk_ref[...].astype(F32)
    new_v = nv_ref[...].astype(F32)
    where = lax.broadcasted_iota(jnp.int32, (qper, positions), 1)
    for i in range(inst):
        q = q_ref[i]
        scores = lax.dot_general(q, ck_ref[i], NT, preferred_element_type=F32) * scale
        live = where < len_ref[i : i + 1, :]
        scores = jnp.where(live, scores, -jnp.inf)
        score_new = jnp.sum(q.astype(F32) * new_k[i : i + 1, :], axis=1, keepdims=True) * scale
        top = jnp.maximum(jnp.max(scores, axis=1, keepdims=True), score_new)
        weights = jnp.where(live, jnp.exp(scores - top), 0.0)
        weight_new = jnp.exp(score_new - top)
        total = jnp.sum(weights, axis=1, keepdims=True) + weight_new
        probs = (weights / total).astype(BF16)
        prob_new = (weight_new / total).astype(BF16).astype(F32)
        mixed = jnp.dot(probs, cv_ref[i], preferred_element_type=F32)
        mix[i] = mixed + prob_new * new_v[i : i + 1, :]
    e = lax.broadcasted_iota(jnp.int32, (GROUP, GROUP), 0)
    c = lax.broadcasted_iota(jnp.int32, (GROUP, GROUP), 1)
    from_e = jnp.where(c < GROUP // 2, 2 * c, 2 * c - GROUP + 1)
    perm = jnp.where(e == from_e, 1.0, 0.0).astype(BF16)
    hq = qper // 2
    for k in range(hq):
        lo = jnp.dot(mix[:, k, :].astype(BF16), perm, preferred_element_type=F32)
        hi = jnp.dot(mix[:, hq + k, :].astype(BF16), perm, preferred_element_type=F32)
        att_mine[:, k * GROUP : (k + 1) * GROUP] = jnp.concatenate([lo, hi], axis=0).astype(BF16)

    pl.semaphore_wait(barrier, 2 * heads - 1)

    def att_copy(i):
        other = lax.rem(head + i, heads)
        return pltpu.make_async_remote_copy(
            src_ref=att_mine,
            dst_ref=att_all.at[head],
            send_sem=att_ss.at[i],
            recv_sem=att_rs.at[head],
            device_id={"head": other, "batch": batch},
            device_id_type=MESH,
        )

    def att_arrival(i):
        other = lax.rem(head + i, heads)
        return pltpu.make_async_remote_copy(
            src_ref=att_mine,
            dst_ref=att_all.at[other],
            send_sem=att_ss.at[i],
            recv_sem=att_rs.at[other],
            device_id={"head": other, "batch": batch},
            device_id_type=MESH,
        )

    def att_start(i, _):
        att_copy(i).start()
        return 0

    lax.fori_loop(1, heads, att_start, 0)
    att_all[head] = att_mine[...]

    osf[...] = os_ref[...].astype(F32)
    gsf[...] = gs_ref[...].astype(F32)
    usf[...] = us_ref[...].astype(F32)
    dsf[...] = ds_ref[...].astype(F32)
    hg = GROUP // 2

    def out_unpack(c, _):
        out_copy(c).wait()
        slot = lax.rem(c, out_slots)
        for s in range(CHUNK // hg):
            w = oring[slot, s * hg : (s + 1) * hg, :]
            g = c * (CHUNK // hg) + s
            ocodes[g, 0:hg, :] = (w & 15).astype(F32).astype(BF16)
            ocodes[g, hg:GROUP, :] = (w >> 4).astype(F32).astype(BF16)

        @pl.when(c + out_slots < out_chunks)
        def _():
            out_copy(c + out_slots).start()

        return 0

    lax.fori_loop(0, out_chunks, out_unpack, 0)

    def att_wait(i, _):
        att_copy(i).wait_send()
        att_arrival(i).wait_recv()
        return 0

    lax.fori_loop(1, heads, att_wait, 0)

    for unit in range(heads):
        block, g = unit // KV_HEADS, unit % KV_HEADS
        tile = att_all[unit].astype(F32)
        for k in range(qper):
            part = tile[(k // hq) * inst : (k // hq + 1) * inst, (k % hq) * GROUP : (k % hq + 1) * GROUP]
            att_lhs[g * qper + k, block * inst : (block + 1) * inst, :] = part

    def project(gg, total):
        for s in range(2):
            g = gg * 2 + s
            lhs = att_lhs[g]
            p = jnp.dot(lhs.astype(BF16), ocodes[g], preferred_element_type=F32)
            corr = 8.0 * jnp.sum(lhs, axis=1, keepdims=True)
            total = total + osf[pl.ds(g, 1), :] * (p - corr)
        return total

    projected = lax.fori_loop(0, 2 * words // GROUP // 2, project, jnp.zeros((rows, width), F32))
    stream = (res_ref[...] + projected).astype(BF16)
    stream_ref[...] = stream
    stream_f = stream.astype(F32)
    sq_mine[...] = jnp.broadcast_to(
        jnp.sum(stream_f * stream_f, axis=1, keepdims=True), sq_mine.shape
    )
    x_mine[...] = stream_f * gain_ref[...]

    owner = head // half
    place = batch * half + lax.rem(head, half)

    def x_copy(i):
        other = lax.rem(head + i, heads)
        return pltpu.make_async_remote_copy(
            src_ref=x_mine,
            dst_ref=x_all.at[place],
            send_sem=x_ss.at[i],
            recv_sem=x_rs.at[place],
            device_id={"head": other, "batch": owner},
            device_id_type=MESH,
        )

    def sq_copy(i):
        other = lax.rem(head + i // 2, heads)
        other_b = lax.rem(batch + i, 2)
        return pltpu.make_async_remote_copy(
            src_ref=sq_mine,
            dst_ref=sq_all.at[batch * heads + head],
            send_sem=sq_ss.at[i],
            recv_sem=sq_rs.at[batch * heads + head],
            device_id={"head": other, "batch": other_b},
            device_id_type=MESH,
        )

    def x_start(i, _):
        @pl.when(jnp.logical_or(i > 0, owner != batch))
        def _():
            x_copy(i).start()

        return 0

    def sq_start(i, _):
        sq_copy(i).start()
        return 0

    lax.fori_loop(0, heads, x_start, 0)
    lax.fori_loop(1, 2 * heads, sq_start, 0)

    @pl.when(owner == batch)
    def _():
        x_all[place] = x_mine[...]

    sq_all[batch * heads + head] = sq_mine[...]

    def x_wait_send(i, _):
        @pl.when(jnp.logical_or(i > 0, owner != batch))
        def _():
            x_copy(i).wait_send()

        return 0

    def x_wait(p, _):
        @pl.when(jnp.logical_or(p != place, owner != batch))
        def _():
            pltpu.make_async_remote_copy(
                src_ref=x_mine,
                dst_ref=x_all.at[p],
                send_sem=x_ss.at[0],
                recv_sem=x_rs.at[p],
                device_id={"head": head, "batch": 1 - batch},
                device_id_type=MESH,
            ).wait_recv()

        return 0

    def sq_wait_send(i, _):
        sq_copy(i).wait_send()
        return 0

    def sq_wait(p, _):
        @pl.when(p != batch * heads + head)
        def _():
            pltpu.make_async_remote_copy(
                src_ref=sq_mine,
                dst_ref=sq_all.at[p],
                send_sem=sq_ss.at[0],
                recv_sem=sq_rs.at[p],
                device_id={"head": head, "batch": 1 - batch},
                device_id_type=MESH,
            ).wait_recv()

        return 0

    lax.fori_loop(0, heads, x_wait_send, 0)
    lax.fori_loop(1, 2 * heads, sq_wait_send, 0)
    lax.fori_loop(0, heads, x_wait, 0)
    lax.fori_loop(0, 2 * heads, sq_wait, 0)

    roots = []
    for b in range(2):
        squares = sq_all[b * heads]
        for h in range(1, heads):
            squares = squares + sq_all[b * heads + h]
        roots.append(lax.rsqrt(squares / (width * heads) + EPSILON))
    zeros = jnp.zeros((both, GROUP), BF16)
    for g in range(feat // GROUP):
        hh, off = g * GROUP // width, g * GROUP % width
        pieces = [x_all[b * half + hh, :, off : off + GROUP] * roots[b] for b in range(2)]
        x = jnp.concatenate(pieces, axis=0).astype(BF16)
        kp, odd = g // 2, g % 2
        lanes = slice(odd * GROUP, (odd + 1) * GROUP)
        nbd[kp, odd * both : (odd + 1) * both, lanes] = x
        nbd[kp, (1 - odd) * both : (2 - odd) * both, lanes] = zeros
        nsum[g] = jnp.broadcast_to(
            8.0 * jnp.sum(x.astype(F32), axis=1, keepdims=True), (both, GROUP)
        )

    acc_out[...] = jnp.zeros_like(acc_out)

    def part_copy(j):
        return pltpu.make_async_remote_copy(
            src_ref=part_send.at[j],
            dst_ref=part_recv.at[j],
            send_sem=pt_ss.at[j],
            recv_sem=pt_rs.at[j],
            device_id={"head": head, "batch": 1 - batch},
            device_id_type=MESH,
        )

    def down(j):
        slot = lax.rem(j, 2)
        part_copy(j).wait()
        gate = acc[slot, 0] + part_recv[j, 0].astype(F32)
        up = acc[slot, 1] + part_recv[j, 1].astype(F32)
        hidden = (gate / (1.0 + jnp.exp(-gate)) * up).astype(BF16)
        lhs, corr = [], []
        for pp in range(FTILE // 256):
            h0 = hidden[:, pp * 256 : pp * 256 + GROUP]
            h1 = hidden[:, pp * 256 + GROUP : (pp + 1) * 256]
            lhs.append(
                jnp.concatenate(
                    [jnp.concatenate([h0, zeros], axis=1), jnp.concatenate([zeros, h1], axis=1)],
                    axis=0,
                )
            )
            for h in (h0, h1):
                corr.append(8.0 * jnp.sum(h.astype(F32), axis=1, keepdims=True))

        def dchunk(n, _):
            first = pl.multiple_of(n * CHUNK, CHUNK)
            total = acc_out[:, pl.ds(first, CHUNK)]
            for pp in range(FTILE // 256):
                codes = dcodes[slot, pl.ds(first, CHUNK), pp * 256 : (pp + 1) * 256]
                p = lax.dot_general(lhs[pp], codes, NT, preferred_element_type=F32)
                for s in range(2):
                    g = j * (FTILE // GROUP) + pp * 2 + s
                    row = dsf[pl.ds(g, 1), pl.ds(first, CHUNK)]
                    total = total + row * (p[s * both : (s + 1) * both] - corr[pp * 2 + s])
            acc_out[:, pl.ds(first, CHUNK)] = total
            return 0

        lax.fori_loop(0, feat // CHUNK, dchunk, 0)

    def ftile(j, _):
        slot = lax.rem(j, 2)
        acc[slot] = jnp.zeros(acc.shape[1:], F32)

        def chunk(k, _):
            c = j * kchunks + k
            rslot = lax.rem(c, ffn_slots)
            ffn_copy(c).wait()
            lhs = nbd[k]
            n0 = jnp.concatenate([nsum[2 * k]] * 2, axis=1)
            n1 = jnp.concatenate([nsum[2 * k + 1]] * 2, axis=1)
            for n in range(FTILE // 256):
                cols = slice(n * 256, (n + 1) * 256)
                w = fring[rslot, :, cols]
                at = pl.ds(pl.multiple_of(j * FTILE + n * 256, 256), 256)
                dcodes[slot, pl.ds(pl.multiple_of(k * CHUNK, CHUNK), CHUNK), cols] = (
                    (w >> 8).astype(F32).astype(BF16)
                )
                for which, scales in ((0, gsf), (1, usf)):
                    bits = (w & 15) if which == 0 else ((w >> 4) & 15)
                    p = jnp.dot(lhs, bits.astype(F32).astype(BF16), preferred_element_type=F32)
                    acc[slot, which, :, cols] += (
                        scales[pl.ds(2 * k, 1), at] * (p[:both] - n0)
                        + scales[pl.ds(2 * k + 1, 1), at] * (p[both:] - n1)
                    )

            @pl.when(c + ffn_slots < total_chunks)
            def _():
                ffn_copy(c + ffn_slots).start()

            return 0

        lax.fori_loop(0, kchunks, chunk, 0)
        part_send[j] = acc[slot].astype(BF16)
        part_copy(j).start()

        @pl.when(j > 0)
        def _():
            down(j - 1)

        return 0

    lax.fori_loop(0, ftiles, ftile, 0)
    down(ftiles - 1)

    share = out_ref.shape[1]
    for t in range(heads):
        rs_send[t] = acc_out[:, t * share : (t + 1) * share].astype(BF16)

    def rs_copy(i):
        other = lax.rem(head + i, heads)
        return pltpu.make_async_remote_copy(
            src_ref=rs_send.at[other],
            dst_ref=rs_recv.at[head],
            send_sem=rd_ss.at[i],
            recv_sem=rd_rs.at[head],
            device_id={"head": other, "batch": batch},
            device_id_type=MESH,
        )

    def rs_start(i, _):
        rs_copy(i).start()
        return 0

    lax.fori_loop(1, heads, rs_start, 0)
    rs_recv[head] = rs_send[head]

    def rs_wait(i, _):
        other = lax.rem(head + i, heads)
        rs_copy(i).wait_send()
        pltpu.make_async_remote_copy(
            src_ref=rs_send.at[other],
            dst_ref=rs_recv.at[other],
            send_sem=rd_ss.at[i],
            recv_sem=rd_rs.at[other],
            device_id={"head": other, "batch": batch},
            device_id_type=MESH,
        ).wait_recv()
        return 0

    lax.fori_loop(1, heads, rs_wait, 0)
    result = rs_recv[0].astype(F32)
    for t in range(1, heads):
        result = result + rs_recv[t].astype(F32)
    out_ref[...] = result.astype(BF16)


def body(
    residual,
    norm_gain,
    queries,
    cache_keys,
    cache_values,
    new_keys,
    new_values,
    lengths,
    out_packed,
    out_scales,
    ffn_packed,
    gate_scales,
    up_scales,
    down_scales,
):
    micro, _, slots, qper, hd = queries.shape
    heads = lax.axis_size("head")
    positions = cache_keys.shape[3]
    inst = micro * slots
    blocks = residual.shape[1] // slots
    rows = micro * residual.shape[1]
    width = residual.shape[2]
    feat, hidden_units = ffn_packed.shape
    words = out_packed.shape[0]
    both = 2 * rows
    share = feat // heads
    ftiles = hidden_units // FTILE
    unit = lax.axis_index("batch") * heads + lax.axis_index("head")
    first_row = unit // KV_HEADS * slots
    lens = lax.dynamic_slice_in_dim(lengths, first_row, slots, axis=1).reshape(inst, 1)
    lens = jnp.broadcast_to(lens, (inst, positions))
    res = residual.reshape(micro, blocks, slots, width).transpose(1, 0, 2, 3)
    res = res.reshape(rows, width).astype(F32)
    gain = norm_gain.astype(F32).reshape(1, width)
    out_slots = min(8, words // CHUNK)
    ffn_slots = min(16, (feat // CHUNK) * ftiles)
    groups = 2 * words // GROUP
    vmem = pl.BlockSpec(memory_space=pltpu.VMEM)
    anywhere = pl.BlockSpec(memory_space=pl.ANY)
    dma = pltpu.SemaphoreType.DMA
    stream, out = pl.pallas_call(
        functools.partial(kernel, heads, blocks),
        out_shape=(
            jax.ShapeDtypeStruct((rows, width), BF16),
            jax.ShapeDtypeStruct((both, share), BF16),
        ),
        in_specs=[vmem] * 8 + [anywhere, vmem, anywhere, vmem, vmem, vmem],
        out_specs=(vmem, vmem),
        scratch_shapes=[
            pltpu.VMEM((out_slots, CHUNK, width), jnp.int32),
            pltpu.VMEM((groups, GROUP, width), BF16),
            pltpu.VMEM(out_scales.shape, F32),
            pltpu.VMEM(gate_scales.shape, F32),
            pltpu.VMEM(up_scales.shape, F32),
            pltpu.VMEM(down_scales.shape, F32),
            pltpu.VMEM((inst, qper, hd), F32),
            pltpu.VMEM((2 * inst, qper // 2 * hd), BF16),
            pltpu.VMEM((heads, 2 * inst, qper // 2 * hd), BF16),
            pltpu.VMEM((groups, rows, GROUP), F32),
            pltpu.VMEM((rows, width), F32),
            pltpu.VMEM((heads, rows, width), F32),
            pltpu.VMEM((rows, GROUP), F32),
            pltpu.VMEM((2 * heads, rows, GROUP), F32),
            pltpu.VMEM((feat // 256, 2 * both, 256), BF16),
            pltpu.VMEM((feat // GROUP, both, GROUP), F32),
            pltpu.VMEM((ffn_slots, CHUNK, FTILE), jnp.int32),
            pltpu.VMEM((2, feat, FTILE), BF16),
            pltpu.VMEM((2, 2, both, FTILE), F32),
            pltpu.VMEM((ftiles, 2, both, FTILE), BF16),
            pltpu.VMEM((ftiles, 2, both, FTILE), BF16),
            pltpu.VMEM((both, feat), F32),
            pltpu.VMEM((heads, both, share), BF16),
            pltpu.VMEM((heads, both, share), BF16),
            dma((out_slots,)),
            dma((ffn_slots,)),
            dma((heads,)),
            dma((heads,)),
            dma((heads,)),
            dma((heads,)),
            dma((2 * heads,)),
            dma((2 * heads,)),
            dma((ftiles,)),
            dma((ftiles,)),
            dma((heads,)),
            dma((heads,)),
        ],
        compiler_params=pltpu.CompilerParams(
            collective_id=0, has_side_effects=True, vmem_limit_bytes=58 * 1024 * 1024
        ),
    )(
        res,
        gain,
        queries.reshape(inst, qper, hd),
        cache_keys.reshape(inst, positions, hd),
        cache_values.reshape(inst, positions, hd),
        new_keys.reshape(inst, hd),
        new_values.reshape(inst, hd),
        lens,
        out_packed,
        out_scales,
        ffn_packed,
        gate_scales,
        up_scales,
        down_scales,
    )
    stream = stream.reshape(blocks, micro, slots, width).transpose(1, 0, 2, 3)
    stream = stream.reshape(micro, blocks * slots, width)
    out = out.reshape(2, blocks, micro, slots, share).transpose(2, 0, 1, 3, 4)
    out = out.reshape(micro, 2 * blocks * slots, share)
    return (stream, out)


def solution(mesh):
    return jax.shard_map(
        body,
        mesh=mesh,
        in_specs=(
            P(None, ("replica", "batch"), "head"),
            P("head"),
            P(None, ("replica", "batch", "head"), None, None, None),
            P(None, ("replica", "batch", "head"), None, None, None),
            P(None, ("replica", "batch", "head"), None, None, None),
            P(None, ("replica", "batch", "head"), None, None),
            P(None, ("replica", "batch", "head"), None, None),
            P(None, "replica"),
            P(None, "head"),
            P(None, "head"),
            P("batch", "head"),
            P("batch", "head"),
            P("batch", "head"),
            P("head", "batch"),
        ),
        out_specs=(P(None, ("replica", "batch"), "head"), P(None, "replica", ("batch", "head"))),
        check_vma=False,
    )
```

```python
import functools

import jax
import jax.numpy as jnp
from jax import lax
from jax.experimental import pallas as pl
from jax.experimental.pallas import tpu as pltpu
from jax.sharding import PartitionSpec as P

KV_HEADS = 8
GROUP = 128
EPSILON = 1e-05
MESH = pl.DeviceIdType.MESH
F32 = jnp.float32
BF16 = jnp.bfloat16
CHUNK = 256
FTILE = 512
DUNROLL = 16
KUNROLL = 8
PUNROLL = 8
NT = (((1,), (1,)), ((), ()))


def kernel(
    heads,
    blocks,
    res_ref,
    gain_ref,
    q_ref,
    ck_ref,
    cv_ref,
    nk_ref,
    nv_ref,
    len_ref,
    op_ref,
    os_ref,
    fp_ref,
    gs_ref,
    us_ref,
    ds_ref,
    stream_ref,
    out_ref,
    oring,
    ocodes,
    osf,
    gsf,
    usf,
    dsf,
    mix,
    att_mine,
    att_all,
    att_lhs,
    x_mine,
    x_all,
    sq_mine,
    sq_all,
    nbd,
    nsum,
    fring,
    dcodes,
    acc,
    part_send,
    part_recv,
    acc_out,
    rs_send,
    rs_recv,
    osem,
    fsem,
    att_ss,
    att_rs,
    x_ss,
    x_rs,
    sq_ss,
    sq_rs,
    pt_ss,
    pt_rs,
    rd_ss,
    rd_rs,
):
    head = lax.axis_index("head")
    batch = lax.axis_index("batch")
    half = heads // 2
    inst = q_ref.shape[0]
    qper = q_ref.shape[1]
    positions = ck_ref.shape[1]
    rows = blocks * inst
    width = res_ref.shape[2]
    both = 2 * rows
    feat = fp_ref.shape[0]
    hidden_units = fp_ref.shape[1]
    words = op_ref.shape[0]
    out_slots = oring.shape[0]
    ffn_slots = fring.shape[0]
    out_chunks = words // CHUNK
    kchunks = feat // CHUNK
    ftiles = hidden_units // FTILE
    total_chunks = kchunks * ftiles

    def out_copy(c):
        slot = lax.rem(c, out_slots)
        first = pl.multiple_of(c * CHUNK, CHUNK)
        return pltpu.make_async_copy(
            op_ref.at[pl.ds(first, CHUNK), :], oring.at[slot], osem.at[slot]
        )

    def ffn_copy(c):
        slot = lax.rem(c, ffn_slots)
        j = c // kchunks
        k = lax.rem(c, kchunks)
        return pltpu.make_async_copy(
            fp_ref.at[
                pl.ds(pl.multiple_of(k * CHUNK, CHUNK), CHUNK),
                pl.ds(pl.multiple_of(j * FTILE, FTILE), FTILE),
            ],
            fring.at[slot],
            fsem.at[slot],
        )

    def start_out(c, _):
        out_copy(c).start()
        return 0

    def start_ffn(c, _):
        ffn_copy(c).start()
        return 0

    barrier = pltpu.get_barrier_semaphore()

    def greet(i, _):
        other = lax.rem(head + i, heads)
        pl.semaphore_signal(
            barrier, inc=1, device_id={"head": other, "batch": 1 - batch}, device_id_type=MESH
        )

        @pl.when(i > 0)
        def _():
            pl.semaphore_signal(
                barrier, inc=1, device_id={"head": other, "batch": batch}, device_id_type=MESH
            )

        return 0

    lax.fori_loop(0, heads, greet, 0)
    lax.fori_loop(0, out_slots, start_out, 0)
    lax.fori_loop(0, ffn_slots, start_ffn, 0)

    scale = q_ref.shape[2] ** (-0.5)
    new_k = nk_ref[...].astype(F32)
    new_v = nv_ref[...].astype(F32)
    where = lax.broadcasted_iota(jnp.int32, (qper, positions), 1)
    for i in range(inst):
        q = q_ref[i]
        scores = lax.dot_general(q, ck_ref[i], NT, preferred_element_type=F32) * scale
        live = where < len_ref[i : i + 1, :]
        scores = jnp.where(live, scores, -jnp.inf)
        score_new = jnp.sum(q.astype(F32) * new_k[i : i + 1, :], axis=1, keepdims=True) * scale
        top = jnp.maximum(jnp.max(scores, axis=1, keepdims=True), score_new)
        weights = jnp.where(live, jnp.exp(scores - top), 0.0)
        weight_new = jnp.exp(score_new - top)
        total = jnp.sum(weights, axis=1, keepdims=True) + weight_new
        probs = (weights / total).astype(BF16)
        prob_new = (weight_new / total).astype(BF16).astype(F32)
        mixed = jnp.dot(probs, cv_ref[i], preferred_element_type=F32)
        mix[i] = mixed + prob_new * new_v[i : i + 1, :]
    e = lax.broadcasted_iota(jnp.int32, (GROUP, GROUP), 0)
    c = lax.broadcasted_iota(jnp.int32, (GROUP, GROUP), 1)
    from_e = jnp.where(c < GROUP // 2, 2 * c, 2 * c - GROUP + 1)
    perm = jnp.where(e == from_e, 1.0, 0.0).astype(BF16)
    hq = qper // 2
    for k in range(hq):
        lo = jnp.dot(mix[:, k, :].astype(BF16), perm, preferred_element_type=F32)
        hi = jnp.dot(mix[:, hq + k, :].astype(BF16), perm, preferred_element_type=F32)
        att_mine[:, k * GROUP : (k + 1) * GROUP] = jnp.concatenate([lo, hi], axis=0).astype(BF16)

    pl.semaphore_wait(barrier, 2 * heads - 1)

    def att_copy(i):
        other = lax.rem(head + i, heads)
        return pltpu.make_async_remote_copy(
            src_ref=att_mine,
            dst_ref=att_all.at[head],
            send_sem=att_ss.at[i],
            recv_sem=att_rs.at[head],
            device_id={"head": other, "batch": batch},
            device_id_type=MESH,
        )

    def att_arrival(i):
        other = lax.rem(head + i, heads)
        return pltpu.make_async_remote_copy(
            src_ref=att_mine,
            dst_ref=att_all.at[other],
            send_sem=att_ss.at[i],
            recv_sem=att_rs.at[other],
            device_id={"head": other, "batch": batch},
            device_id_type=MESH,
        )

    def att_start(i, _):
        att_copy(i).start()
        return 0

    lax.fori_loop(1, heads, att_start, 0)
    att_all[head] = att_mine[...]

    osf[...] = os_ref[...].astype(F32)
    gsf[...] = gs_ref[...].astype(F32)
    usf[...] = us_ref[...].astype(F32)
    dsf[...] = ds_ref[...].astype(F32)
    hg = GROUP // 2

    def out_unpack(c, _):
        out_copy(c).wait()
        slot = lax.rem(c, out_slots)
        for s in range(CHUNK // hg):
            w = oring[slot, s * hg : (s + 1) * hg, :]
            g = c * (CHUNK // hg) + s
            ocodes[g, 0:hg, :] = (w & 15).astype(F32).astype(BF16)
            ocodes[g, hg:GROUP, :] = (w >> 4).astype(F32).astype(BF16)

        @pl.when(c + out_slots < out_chunks)
        def _():
            out_copy(c + out_slots).start()

        return 0

    lax.fori_loop(0, out_chunks, out_unpack, 0)

    def att_wait(i, _):
        att_copy(i).wait_send()
        att_arrival(i).wait_recv()
        return 0

    lax.fori_loop(1, heads, att_wait, 0)

    for unit in range(heads):
        block, g = unit // KV_HEADS, unit % KV_HEADS
        tile = att_all[unit].astype(F32)
        for k in range(qper):
            part = tile[(k // hq) * inst : (k // hq + 1) * inst, (k % hq) * GROUP : (k % hq + 1) * GROUP]
            att_lhs[g * qper + k, block * inst : (block + 1) * inst, :] = part

    def project(gg, total):
        for s in range(PUNROLL):
            g = gg * PUNROLL + s
            lhs = att_lhs[g]
            p = jnp.dot(lhs.astype(BF16), ocodes[g], preferred_element_type=F32)
            corr = 8.0 * jnp.sum(lhs, axis=1, keepdims=True)
            total = total + osf[pl.ds(g, 1), :] * (p - corr)
        return total

    projected = lax.fori_loop(0, 2 * words // GROUP // PUNROLL, project, jnp.zeros((rows, width), F32))
    micro = res_ref.shape[0]
    slots = inst // micro
    res = [res_ref[m].astype(F32) for m in range(micro)]
    res = [
        res[m][b * slots : (b + 1) * slots] for b in range(blocks) for m in range(micro)
    ]
    stream = (jnp.concatenate(res, axis=0) + projected).astype(BF16)
    stream_f = stream.astype(F32)
    for m in range(micro):
        firsts = [b * inst + m * slots for b in range(blocks)]
        stream_ref[m] = jnp.concatenate(
            [stream_f[first : first + slots] for first in firsts], axis=0
        ).astype(BF16)
    sq_mine[...] = jnp.broadcast_to(
        jnp.sum(stream_f * stream_f, axis=1, keepdims=True), sq_mine.shape
    )
    x_mine[...] = stream_f * gain_ref[...]

    owner = head // half
    place = batch * half + lax.rem(head, half)

    def x_copy(i):
        other = lax.rem(head + i, heads)
        return pltpu.make_async_remote_copy(
            src_ref=x_mine,
            dst_ref=x_all.at[place],
            send_sem=x_ss.at[i],
            recv_sem=x_rs.at[place],
            device_id={"head": other, "batch": owner},
            device_id_type=MESH,
        )

    def sq_copy(i):
        other = lax.rem(head + i // 2, heads)
        other_b = lax.rem(batch + i, 2)
        return pltpu.make_async_remote_copy(
            src_ref=sq_mine,
            dst_ref=sq_all.at[batch * heads + head],
            send_sem=sq_ss.at[i],
            recv_sem=sq_rs.at[batch * heads + head],
            device_id={"head": other, "batch": other_b},
            device_id_type=MESH,
        )

    def x_start(i, _):
        @pl.when(jnp.logical_or(i > 0, owner != batch))
        def _():
            x_copy(i).start()

        return 0

    def sq_start(i, _):
        sq_copy(i).start()
        return 0

    lax.fori_loop(0, heads, x_start, 0)
    lax.fori_loop(1, 2 * heads, sq_start, 0)

    @pl.when(owner == batch)
    def _():
        x_all[place] = x_mine[...]

    sq_all[batch * heads + head] = sq_mine[...]

    def x_wait_send(i, _):
        @pl.when(jnp.logical_or(i > 0, owner != batch))
        def _():
            x_copy(i).wait_send()

        return 0

    def x_wait(p, _):
        @pl.when(jnp.logical_or(p != place, owner != batch))
        def _():
            pltpu.make_async_remote_copy(
                src_ref=x_mine,
                dst_ref=x_all.at[p],
                send_sem=x_ss.at[0],
                recv_sem=x_rs.at[p],
                device_id={"head": head, "batch": 1 - batch},
                device_id_type=MESH,
            ).wait_recv()

        return 0

    def sq_wait_send(i, _):
        sq_copy(i).wait_send()
        return 0

    def sq_wait(p, _):
        @pl.when(p != batch * heads + head)
        def _():
            pltpu.make_async_remote_copy(
                src_ref=sq_mine,
                dst_ref=sq_all.at[p],
                send_sem=sq_ss.at[0],
                recv_sem=sq_rs.at[p],
                device_id={"head": head, "batch": 1 - batch},
                device_id_type=MESH,
            ).wait_recv()

        return 0

    lax.fori_loop(0, heads, x_wait_send, 0)
    lax.fori_loop(1, 2 * heads, sq_wait_send, 0)
    lax.fori_loop(0, heads, x_wait, 0)
    lax.fori_loop(0, 2 * heads, sq_wait, 0)

    roots = []
    for b in range(2):
        squares = sq_all[b * heads]
        for h in range(1, heads):
            squares = squares + sq_all[b * heads + h]
        roots.append(lax.rsqrt(squares / (width * heads) + EPSILON))
    zeros = jnp.zeros((both, GROUP), BF16)
    for g in range(feat // GROUP):
        hh, off = g * GROUP // width, g * GROUP % width
        pieces = [x_all[b * half + hh, :, off : off + GROUP] * roots[b] for b in range(2)]
        x = jnp.concatenate(pieces, axis=0).astype(BF16)
        kp, odd = g // 2, g % 2
        lanes = slice(odd * GROUP, (odd + 1) * GROUP)
        nbd[kp, odd * both : (odd + 1) * both, lanes] = x
        nbd[kp, (1 - odd) * both : (2 - odd) * both, lanes] = zeros
        nsum[g] = jnp.broadcast_to(
            8.0 * jnp.sum(x.astype(F32), axis=1, keepdims=True), (both, GROUP)
        )

    acc_out[...] = jnp.zeros_like(acc_out)

    def part_copy(j):
        return pltpu.make_async_remote_copy(
            src_ref=part_send.at[j],
            dst_ref=part_recv.at[j],
            send_sem=pt_ss.at[j],
            recv_sem=pt_rs.at[j],
            device_id={"head": head, "batch": 1 - batch},
            device_id_type=MESH,
        )

    def down(j):
        slot = lax.rem(j, 2)
        part_copy(j).wait()
        gate = acc[slot, 0] + part_recv[j, 0].astype(F32)
        up = acc[slot, 1] + part_recv[j, 1].astype(F32)
        hidden = (gate / (1.0 + jnp.exp(-gate)) * up).astype(BF16)
        lhs, corr = [], []
        for pp in range(FTILE // 256):
            h0 = hidden[:, pp * 256 : pp * 256 + GROUP]
            h1 = hidden[:, pp * 256 + GROUP : (pp + 1) * 256]
            lhs.append(
                jnp.concatenate(
                    [jnp.concatenate([h0, zeros], axis=1), jnp.concatenate([zeros, h1], axis=1)],
                    axis=0,
                )
            )
            for h in (h0, h1):
                corr.append(8.0 * jnp.sum(h.astype(F32), axis=1, keepdims=True))

        def dchunk(nn, _):
            for u in range(DUNROLL):
                first = pl.multiple_of((nn * DUNROLL + u) * CHUNK, CHUNK)
                total = acc_out[:, pl.ds(first, CHUNK)]
                for pp in range(FTILE // 256):
                    codes = dcodes[slot, pl.ds(first, CHUNK), pp * 256 : (pp + 1) * 256]
                    p = lax.dot_general(lhs[pp], codes, NT, preferred_element_type=F32)
                    for s in range(2):
                        g = j * (FTILE // GROUP) + pp * 2 + s
                        row = dsf[pl.ds(g, 1), pl.ds(first, CHUNK)]
                        total = total + row * (p[s * both : (s + 1) * both] - corr[pp * 2 + s])
                acc_out[:, pl.ds(first, CHUNK)] = total
            return 0

        lax.fori_loop(0, feat // CHUNK // DUNROLL, dchunk, 0)

    def ftile(j, _):
        slot = lax.rem(j, 2)
        acc[slot] = jnp.zeros(acc.shape[1:], F32)

        def chunk(kk, _):
            ks = [kk * KUNROLL + u for u in range(KUNROLL)]
            for k in ks:
                ffn_copy(j * kchunks + k).wait()
            for n in range(FTILE // 256):
                cols = slice(n * 256, (n + 1) * 256)
                at = pl.ds(pl.multiple_of(j * FTILE + n * 256, 256), 256)
                totals = [acc[slot, 0, :, cols], acc[slot, 1, :, cols]]
                for k in ks:
                    rslot = lax.rem(j * kchunks + k, ffn_slots)
                    lhs = nbd[k]
                    n0 = jnp.concatenate([nsum[2 * k]] * 2, axis=1)
                    n1 = jnp.concatenate([nsum[2 * k + 1]] * 2, axis=1)
                    w = fring[rslot, :, cols]
                    dcodes[slot, pl.ds(pl.multiple_of(k * CHUNK, CHUNK), CHUNK), cols] = (
                        (w >> 8).astype(F32).astype(BF16)
                    )
                    sums = [
                        jnp.dot(lhs, (w & most).astype(F32).astype(BF16), preferred_element_type=F32)
                        for most in (15, 255)
                    ]
                    sums[1] = (sums[1] - sums[0]) * 0.0625
                    for which, scales in ((0, gsf), (1, usf)):
                        p = sums[which]
                        totals[which] = totals[which] + (
                            scales[pl.ds(2 * k, 1), at] * (p[:both] - n0)
                            + scales[pl.ds(2 * k + 1, 1), at] * (p[both:] - n1)
                        )
                acc[slot, 0, :, cols] = totals[0]
                acc[slot, 1, :, cols] = totals[1]
            for k in ks:
                c = j * kchunks + k

                @pl.when(c + ffn_slots < total_chunks)
                def _():
                    ffn_copy(c + ffn_slots).start()

            return 0

        lax.fori_loop(0, kchunks // KUNROLL, chunk, 0)
        part_send[j] = acc[slot].astype(BF16)
        part_copy(j).start()

        @pl.when(j > 0)
        def _():
            down(j - 1)

        return 0

    lax.fori_loop(0, ftiles, ftile, 0)
    down(ftiles - 1)

    share = out_ref.shape[2]
    for t in range(heads):
        rs_send[t] = acc_out[:, t * share : (t + 1) * share].astype(BF16)

    def rs_copy(i):
        other = lax.rem(head + i, heads)
        return pltpu.make_async_remote_copy(
            src_ref=rs_send.at[other],
            dst_ref=rs_recv.at[head],
            send_sem=rd_ss.at[i],
            recv_sem=rd_rs.at[head],
            device_id={"head": other, "batch": batch},
            device_id_type=MESH,
        )

    def rs_start(i, _):
        rs_copy(i).start()
        return 0

    lax.fori_loop(1, heads, rs_start, 0)
    rs_recv[head] = rs_send[head]

    def rs_wait(i, _):
        other = lax.rem(head + i, heads)
        rs_copy(i).wait_send()
        pltpu.make_async_remote_copy(
            src_ref=rs_send.at[other],
            dst_ref=rs_recv.at[other],
            send_sem=rd_ss.at[i],
            recv_sem=rd_rs.at[other],
            device_id={"head": other, "batch": batch},
            device_id_type=MESH,
        ).wait_recv()
        return 0

    lax.fori_loop(1, heads, rs_wait, 0)
    result = rs_recv[0].astype(F32)
    for t in range(1, heads):
        result = result + rs_recv[t].astype(F32)
    for m in range(micro):
        firsts = [b * inst + m * slots for b in range(2 * blocks)]
        out_ref[m] = jnp.concatenate(
            [result[first : first + slots] for first in firsts], axis=0
        ).astype(BF16)


def body(
    residual,
    norm_gain,
    queries,
    cache_keys,
    cache_values,
    new_keys,
    new_values,
    lengths,
    out_packed,
    out_scales,
    ffn_packed,
    gate_scales,
    up_scales,
    down_scales,
):
    micro, _, slots, qper, hd = queries.shape
    heads = lax.axis_size("head")
    positions = cache_keys.shape[3]
    inst = micro * slots
    blocks = residual.shape[1] // slots
    rows = micro * residual.shape[1]
    width = residual.shape[2]
    feat, hidden_units = ffn_packed.shape
    words = out_packed.shape[0]
    both = 2 * rows
    share = feat // heads
    ftiles = hidden_units // FTILE
    unit = lax.axis_index("batch") * heads + lax.axis_index("head")
    first_row = unit // KV_HEADS * slots
    lens = lax.dynamic_slice_in_dim(lengths, first_row, slots, axis=1).reshape(inst, 1)
    lens = jnp.broadcast_to(lens, (inst, positions))
    gain = norm_gain.astype(F32).reshape(1, width)
    out_slots = min(8, words // CHUNK)
    ffn_slots = min(16, (feat // CHUNK) * ftiles)
    groups = 2 * words // GROUP
    vmem = pl.BlockSpec(memory_space=pltpu.VMEM)
    anywhere = pl.BlockSpec(memory_space=pl.ANY)
    dma = pltpu.SemaphoreType.DMA
    stream, out = pl.pallas_call(
        functools.partial(kernel, heads, blocks),
        out_shape=(
            jax.ShapeDtypeStruct(residual.shape, BF16),
            jax.ShapeDtypeStruct((micro, 2 * blocks * slots, share), BF16),
        ),
        in_specs=[vmem] * 8 + [anywhere, vmem, anywhere, vmem, vmem, vmem],
        out_specs=(vmem, vmem),
        scratch_shapes=[
            pltpu.VMEM((out_slots, CHUNK, width), jnp.int32),
            pltpu.VMEM((groups, GROUP, width), BF16),
            pltpu.VMEM(out_scales.shape, F32),
            pltpu.VMEM(gate_scales.shape, F32),
            pltpu.VMEM(up_scales.shape, F32),
            pltpu.VMEM(down_scales.shape, F32),
            pltpu.VMEM((inst, qper, hd), F32),
            pltpu.VMEM((2 * inst, qper // 2 * hd), BF16),
            pltpu.VMEM((heads, 2 * inst, qper // 2 * hd), BF16),
            pltpu.VMEM((groups, rows, GROUP), F32),
            pltpu.VMEM((rows, width), F32),
            pltpu.VMEM((heads, rows, width), F32),
            pltpu.VMEM((rows, GROUP), F32),
            pltpu.VMEM((2 * heads, rows, GROUP), F32),
            pltpu.VMEM((feat // 256, 2 * both, 256), BF16),
            pltpu.VMEM((feat // GROUP, both, GROUP), F32),
            pltpu.VMEM((ffn_slots, CHUNK, FTILE), jnp.int32),
            pltpu.VMEM((2, feat, FTILE), BF16),
            pltpu.VMEM((2, 2, both, FTILE), F32),
            pltpu.VMEM((ftiles, 2, both, FTILE), BF16),
            pltpu.VMEM((ftiles, 2, both, FTILE), BF16),
            pltpu.VMEM((both, feat), F32),
            pltpu.VMEM((heads, both, share), BF16),
            pltpu.VMEM((heads, both, share), BF16),
            dma((out_slots,)),
            dma((ffn_slots,)),
            dma((heads,)),
            dma((heads,)),
            dma((heads,)),
            dma((heads,)),
            dma((2 * heads,)),
            dma((2 * heads,)),
            dma((ftiles,)),
            dma((ftiles,)),
            dma((heads,)),
            dma((heads,)),
        ],
        compiler_params=pltpu.CompilerParams(
            collective_id=0, has_side_effects=True, vmem_limit_bytes=58 * 1024 * 1024
        ),
    )(
        residual,
        gain,
        queries.reshape(inst, qper, hd),
        cache_keys.reshape(inst, positions, hd),
        cache_values.reshape(inst, positions, hd),
        new_keys.reshape(inst, hd),
        new_values.reshape(inst, hd),
        lens,
        out_packed,
        out_scales,
        ffn_packed,
        gate_scales,
        up_scales,
        down_scales,
    )
    return (stream, out)


def solution(mesh):
    return jax.shard_map(
        body,
        mesh=mesh,
        in_specs=(
            P(None, ("replica", "batch"), "head"),
            P("head"),
            P(None, ("replica", "batch", "head"), None, None, None),
            P(None, ("replica", "batch", "head"), None, None, None),
            P(None, ("replica", "batch", "head"), None, None, None),
            P(None, ("replica", "batch", "head"), None, None),
            P(None, ("replica", "batch", "head"), None, None),
            P(None, "replica"),
            P(None, "head"),
            P(None, "head"),
            P("batch", "head"),
            P("batch", "head"),
            P("batch", "head"),
            P("head", "batch"),
        ),
        out_specs=(P(None, ("replica", "batch"), "head"), P(None, "replica", ("batch", "head"))),
        check_vma=False,
    )
```
